32 devices in a mesh: groups: 2 (over y), path: 4 (over z), inner: 2 (over x), shard: 2 (over core).
Axes of the slice: x: 2, y: 2, z: 4, core: 2. Of those that a mesh axis runs over, the one named last changes fastest.
Arguments:
- route: int32 [8], P('groups'), parts along dimension 0, may hold values from 0 to 7, as said below
- inputs: bfloat16 [8, 512, 2048], P(('groups', 'path'), 'inner'), parts along dimension 0, may hold values from -6 to 6
- targets: bfloat16 [8, 512, 2048], P(('groups', 'path'), 'inner', 'shard'), parts along dimension 0, may hold values from -6 to 6
- path_weights: bfloat16 [8, 2048, 2048], P(('groups', 'path'), 'inner', 'shard'), parts along dimension 0, may hold values from -6 to 6
- momentum: float32 [16, 2, 1024, 2048], P('groups', 'inner', 'path', 'shard'), parts along dimension 0, may hold values from -2 to 2
Outputs:
- new_weights: bfloat16 [8, 2048, 2048], P(('groups', 'path'), 'inner', 'shard'), parts along dimension 0
- new_momentum: float32 [16, 2, 1024, 2048], P('groups', 'inner', 'path', 'shard'), parts along dimension 0
The draws below stay inside these ranges and needn't reach their ends.
There are 2 independent parts, one for each index of `groups`. The reference program is written for one: setup_inputs(seed, part) draws one part's arguments, and reference() takes and returns one part's arrays. A program takes and returns all parts, laid end to end along the dimension named above; each array names one. Nothing has to cross between parts.
Inputs may be any that keep to these rules, and one draw needn't show every extreme that they name: `route`: where 4 >= 8, every module is used by at least one path; where 4 <= 8, the paths use 4 different modules.
All inputs are finite; a program needn't handle non-finite values.
Results may differ from the reference program's by a relative error of at most 0.0055.
Values may be sent and summed in bfloat16 or wider, within the bound.
A program may use at most 128 MiB of HBM per device.

```python
import jax
import jax.numpy as jnp
from jax import lax

D = 2048
M = 8
PATHS = 4
TOK_PATH = 512
N_INNER = 2


def draw_route(key, part):
    key = jax.random.fold_in(key, 7)
    keys = jax.random.split(key, 5)
    order = jax.random.permutation(keys[0], M)
    first = jax.random.randint(keys[1], (PATHS,), 0, M)
    second = jax.random.randint(keys[2], (PATHS,), 0, M)
    third = jax.random.randint(keys[3], (PATHS,), 0, M)
    picked = jnp.minimum(jnp.minimum(first, second), third)
    chosen = order[picked]
    covered = min(M, PATHS)
    spots = jax.random.permutation(keys[4], PATHS)[:covered]
    chosen = chosen.at[spots].set(order[:covered])
    return chosen.astype(jnp.int32)


def shard_levels(rng, dims, cuts, least, largest):
    def one(axis_at, parts):
        steps = jax.random.uniform(jax.random.fold_in(jax.random.fold_in(rng, 6), axis_at), (parts,), jnp.float32, least / len(cuts), largest / len(cuts))
        return jnp.repeat(jnp.exp(steps), dims[axis_at] // parts).reshape((-1,) + (1,) * (len(dims) - axis_at - 1))

    gain = one(*cuts[0])
    for cut in cuts[1:]:
        gain = gain * one(*cut)
    return gain


def centred(key, shape, width, most, pieces=(), kind=jnp.bfloat16):
    array = jax.random.normal(key, shape, jnp.float32) * width
    if len(pieces) > 0:
        array = shard_levels(key, shape, pieces, -0.22, 0.18) * array
    return jnp.clip(array, min=-most, max=most).astype(kind)


def setup_inputs(seed: int = 0, part: int = 0) -> dict:
    arg_keys = jax.random.split(jax.random.key(seed), 6)
    part_keys = jax.random.split(jax.random.fold_in(arg_keys[5], part), 6)
    return {
        "route": draw_route(jax.random.fold_in(jax.random.fold_in(arg_keys[5], part), 71), part),
        "inputs": centred(part_keys[1], (PATHS, TOK_PATH, D), 1.0, 6.0, ((0, 4), (1, 2))),
        "targets": centred(part_keys[2], (PATHS, TOK_PATH, D), 1.0, 6.0, ((0, 4), (1, 2), (2, 2))),
        "path_weights": centred(part_keys[3], (PATHS, D, D), 1.0, 6.0, ((0, 4), (1, 2), (2, 2))),
        "momentum": centred(part_keys[4], (M, N_INNER, D // N_INNER, D), 0.3, 2.0, ((1, 2), (2, 4), (3, 2)), jnp.float32),
    }


eps = 1e-06
inner_rate = 256.0
outer_rate = 0.7
outer_mu = 0.9

def reference(route, inputs, targets, path_weights, momentum):
    scale = D ** (-0.5)
    coef = inner_rate * scale / TOK_PATH
    xf = inputs.astype(jnp.float32)
    normed = (xf * lax.rsqrt(lax.optimization_barrier(jnp.mean(xf * xf, axis=-1, keepdims=True)) + eps)).astype(jnp.bfloat16)

    def path_delta(items):
        z_path, w_path, t_path = items
        output = jnp.dot(z_path, w_path, preferred_element_type=jnp.float32) * scale
        resid = (output - t_path.astype(jnp.float32)).astype(jnp.bfloat16)
        grad = jnp.dot(z_path.T, resid, preferred_element_type=jnp.float32)
        return (grad * coef).astype(jnp.bfloat16)
    delta = lax.map(path_delta, (normed, path_weights, targets))
    onehot = (route[:, None] == jnp.arange(M, dtype=jnp.int32)[None, :]).astype(jnp.float32)
    counts = lax.optimization_barrier(jnp.sum(onehot, axis=0))
    summed = jnp.einsum('pm,prc->mrc', onehot, delta.astype(jnp.float32))
    mean_delta = summed / jnp.maximum(counts, 1.0)[:, None, None]
    velocity = momentum.reshape(M, D, D)
    new_velocity = outer_mu * velocity + mean_delta
    update = (outer_rate * (mean_delta + outer_mu * new_velocity)).astype(jnp.bfloat16)
    chosen = update.astype(jnp.float32)[route]
    new_weights = (path_weights.astype(jnp.float32) - chosen).astype(jnp.bfloat16)
    return (new_weights, new_velocity.reshape(momentum.shape))
```

```python
import functools

import jax
import jax.numpy as jnp
from jax import lax
from jax.experimental import pallas as pl
from jax.experimental.pallas import tpu as pltpu
from jax.sharding import PartitionSpec as P

eps = 1e-06
inner_rate = 256.0
outer_rate = 0.7
outer_mu = 0.9


def per_device(route, inputs, targets, path_weights, momentum):
    n_path = lax.axis_size("path")
    tokens = inputs[0]
    target = targets[0]
    weight = path_weights[0]
    width = tokens.shape[1]
    scale = width ** (-0.5)
    xf = tokens.astype(jnp.float32)
    normed = (xf * lax.rsqrt(jnp.mean(xf * xf, axis=-1, keepdims=True) + eps)).astype(jnp.bfloat16)
    normed_cols = lax.all_to_all(normed, "inner", split_axis=1, concat_axis=0, tiled=True)
    tok_path = normed_cols.shape[0]
    coef = inner_rate * scale / tok_path
    output = jnp.dot(
        normed,
        lax.all_gather(weight, "inner", axis=0, tiled=True),
        preferred_element_type=jnp.float32,
    )
    resid = (output * scale - target.astype(jnp.float32)).astype(jnp.bfloat16)
    grad = lax.dot_general(
        normed_cols,
        lax.all_gather(resid, "inner", axis=0, tiled=True),
        (((0,), (0,)), ((), ())),
        preferred_element_type=jnp.float32,
    )
    delta = (grad * coef).astype(jnp.bfloat16)
    blocks = delta.reshape(n_path, weight.shape[0] // n_path, weight.shape[1])
    received = lax.all_to_all(blocks, "path", split_axis=0, concat_axis=0, tiled=True)
    modules = momentum.shape[0]
    onehot = (route[:, None] == jnp.arange(modules, dtype=jnp.int32)[None, :]).astype(jnp.bfloat16)
    counts = jnp.sum(onehot.astype(jnp.float32), axis=0)
    summed = jnp.einsum("pm,prc->mrc", onehot, received, preferred_element_type=jnp.float32)
    mean_delta = summed / jnp.maximum(counts, 1.0)[:, None, None]
    new_velocity = outer_mu * momentum[:, 0] + mean_delta
    update = (outer_rate * (mean_delta + outer_mu * new_velocity)).astype(jnp.bfloat16)
    outgoing = jnp.einsum("pm,mrc->prc", onehot, update, preferred_element_type=jnp.float32).astype(
        jnp.bfloat16
    )
    returned = lax.all_to_all(outgoing, "path", split_axis=0, concat_axis=0, tiled=True)
    returned = returned.reshape(weight.shape[0], weight.shape[1])
    new_weight = (weight.astype(jnp.float32) - returned.astype(jnp.float32)).astype(jnp.bfloat16)
    return (new_weight[None], new_velocity[:, None])


def select_kernel(route_ref, momentum_ref, out_ref):
    out_ref[...] = momentum_ref[...].astype(out_ref.dtype)


def select_momentum(route, momentum):
    n_path = route.shape[0]
    _, rows, cols = momentum.shape
    return pl.pallas_call(
        select_kernel,
        out_shape=jax.ShapeDtypeStruct((n_path, rows, cols), jnp.bfloat16),
        grid_spec=pltpu.PrefetchScalarGridSpec(
            num_scalar_prefetch=1,
            grid=(n_path,),
            in_specs=[pl.BlockSpec((1, rows, cols), lambda p, route: (route[p], 0, 0))],
            out_specs=pl.BlockSpec((1, rows, cols), lambda p, route: (p, 0, 0)),
        ),
        compiler_params=pltpu.CompilerParams(vmem_limit_bytes=32 * 2**20),
        cost_estimate=pl.CostEstimate(flops=0, bytes_accessed=n_path * rows * cols * 6, transcendentals=0),
    )(route, momentum)


def momentum_kernel(slot_ref, used_ref, momentum_ref, delta_ref, out_ref):
    used = used_ref[pl.program_id(0)]

    @pl.when(used != 0)
    def _():
        out_ref[...] = outer_mu * momentum_ref[...] + delta_ref[...].astype(jnp.float32)

    @pl.when(used == 0)
    def _():
        out_ref[...] = outer_mu * momentum_ref[...]


def next_momentum(route, momentum, received):
    modules, rows, cols = momentum.shape
    hit = route[:, None] == jnp.arange(modules, dtype=jnp.int32)[None, :]
    used = jnp.any(hit, axis=0).astype(jnp.int32)
    slot = jnp.argmax(hit, axis=0).astype(jnp.int32)
    return pl.pallas_call(
        momentum_kernel,
        out_shape=jax.ShapeDtypeStruct((modules, rows, cols), jnp.float32),
        grid_spec=pltpu.PrefetchScalarGridSpec(
            num_scalar_prefetch=2,
            grid=(modules,),
            in_specs=[
                pl.BlockSpec((1, rows, cols), lambda m, slot, used: (m, 0, 0)),
                pl.BlockSpec((1, rows, cols), lambda m, slot, used: (slot[m], 0, 0)),
            ],
            out_specs=pl.BlockSpec((1, rows, cols), lambda m, slot, used: (m, 0, 0)),
        ),
        compiler_params=pltpu.CompilerParams(vmem_limit_bytes=32 * 2**20),
        cost_estimate=pl.CostEstimate(flops=0, bytes_accessed=modules * rows * cols * 9, transcendentals=0),
    )(slot, used, momentum, received)


def sync_kernel(
    n_path,
    chunks,
    x_hbm,
    t_hbm,
    w_hbm,
    m_hbm,
    new_w_hbm,
    recv_hbm,
    x_v,
    t_v,
    w_v,
    nsend,
    ncols,
    psend,
    precv,
    lp,
    resid,
    delta,
    mom,
    load_sem,
    out_sem,
    x_send,
    x_recv,
    m_send,
    m_recv,
    d_send,
    d_recv,
):
    f32 = jnp.float32
    tokens, width = x_v.shape
    rows, cols = w_v.shape
    block = rows // n_path
    step = tokens // chunks
    tile = min(256, cols)
    scale = width ** (-0.5)
    coef = inner_rate * scale / (2 * tokens)
    me = lax.axis_index("path")
    mine = lax.axis_index("inner")
    other = 1 - mine

    load_x = pltpu.make_async_copy(x_hbm, x_v, load_sem.at[0])
    load_w = pltpu.make_async_copy(w_hbm, w_v, load_sem.at[1])
    load_t = pltpu.make_async_copy(t_hbm, t_v, load_sem.at[2])
    load_m = pltpu.make_async_copy(m_hbm.at[me], mom.at[me], load_sem.at[3])
    load_x.start()
    load_w.start()
    load_t.start()
    load_m.start()

    barrier = pltpu.get_barrier_semaphore()
    pl.semaphore_signal(barrier, inc=1, device_id={"inner": other}, device_id_type=pl.DeviceIdType.MESH)
    for d in range(1, n_path):
        pl.semaphore_signal(
            barrier, inc=1, device_id={"path": lax.rem(me + d, n_path)}, device_id_type=pl.DeviceIdType.MESH
        )
    pl.semaphore_wait(barrier, n_path)

    def far(d, src, dst, send, recv):
        return pltpu.make_async_remote_copy(
            src_ref=src,
            dst_ref=dst,
            send_sem=send.at[d - 1],
            recv_sem=recv.at[d - 1],
            device_id={"path": lax.rem(me + d, n_path)},
            device_id_type=pl.DeviceIdType.MESH,
        )

    def near(hop, c, src, dst):
        return pltpu.make_async_remote_copy(
            src_ref=src,
            dst_ref=dst,
            send_sem=x_send.at[hop, c],
            recv_sem=x_recv.at[hop, c],
            device_id={"inner": other},
            device_id_type=pl.DeviceIdType.MESH,
        )

    mom_copies = [far(d, m_hbm.at[lax.rem(me + d, n_path)], mom.at[me], m_send, m_recv) for d in range(1, n_path)]
    for copy in mom_copies:
        copy.start()

    load_x.wait()
    piece = 32
    own_at = pl.ds(pl.multiple_of(mine * rows, rows), rows)
    other_at = pl.ds(pl.multiple_of(other * rows, rows), rows)
    hop0 = []
    for c in range(chunks):

        @pl.loop(0, step // piece)
        def _(k, c=c):
            at = pl.ds(pl.multiple_of(c * step + k * piece, piece), piece)
            xf = x_v[at, :].astype(f32)
            inv = lax.rsqrt(jnp.mean(xf * xf, axis=-1, keepdims=True) + eps)
            ncols[at, :] = (x_v[at, own_at].astype(f32) * inv).astype(jnp.bfloat16)
            nsend[at, :] = (x_v[at, other_at].astype(f32) * inv).astype(jnp.bfloat16)

        at = pl.ds(c * step, step)
        copy = near(0, c, nsend.at[at], ncols.at[pl.ds(tokens + c * step, step)])
        copy.start()
        hop0.append(copy)

    load_w.wait()
    load_t.wait()

    @pl.loop(0, cols // tile)
    def _(j):
        at = pl.ds(pl.multiple_of(j * tile, tile), tile)
        part = jnp.dot(ncols[0:tokens, :], w_v[:, at], preferred_element_type=f32)
        lp[:, at] = part * scale - t_v[:, at].astype(f32)

    hop1 = []
    for c in range(chunks):
        hop0[c].wait_recv()

        @pl.loop(0, cols // tile)
        def _(j, c=c):
            at = pl.ds(pl.multiple_of(j * tile, tile), tile)
            part = jnp.dot(
                ncols[tokens + c * step : tokens + (c + 1) * step, :], w_v[:, at], preferred_element_type=f32
            )
            psend[c * step : (c + 1) * step, at] = (part * scale).astype(jnp.bfloat16)

        at = pl.ds(c * step, step)
        copy = near(1, c, psend.at[at], precv.at[at])
        copy.start()
        hop1.append(copy)

    hop2 = []
    for c in range(chunks):
        hop1[c].wait_recv()

        @pl.loop(0, step // piece)
        def _(k, c=c):
            at = pl.ds(pl.multiple_of(c * step + k * piece, piece), piece)
            resid[at, :] = (lp[at, :] + precv[at, :].astype(f32)).astype(jnp.bfloat16)

        copy = near(2, c, resid.at[pl.ds(c * step, step)], resid.at[pl.ds(tokens + c * step, step)])
        copy.start()
        hop2.append(copy)
    for copy in hop2:
        copy.wait_recv()

    delta_copies = []
    for d in list(range(1, n_path)) + [0]:
        q = lax.rem(me + d, n_path)
        left = pl.ds(pl.multiple_of(q * block, block), block)

        @pl.loop(0, cols // tile)
        def _(j, q=q, left=left):
            at = pl.ds(pl.multiple_of(j * tile, tile), tile)
            grad = lax.dot_general(
                ncols[:, left], resid[:, at], (((0,), (0,)), ((), ())), preferred_element_type=f32
            )
            delta[q, :, at] = (grad * coef).astype(jnp.bfloat16)

        if d > 0:
            copy = far(d, delta.at[q], recv_hbm.at[me], d_send, d_recv)
        else:
            copy = pltpu.make_async_copy(delta.at[q], recv_hbm.at[me], out_sem.at[0])
        copy.start()
        delta_copies.append(copy)

    out_copies = []
    for d in range(n_path):
        if d == 0:
            load_m.wait()
        else:
            mom_copies[d - 1].wait_recv()
        o = lax.rem(me + n_path - d, n_path)

        @pl.loop(0, block // piece)
        def _(k, o=o):
            at = pl.ds(pl.multiple_of(k * piece, piece), piece)
            w_at = pl.ds(pl.multiple_of(o * block + k * piece, piece), piece)
            step_delta = delta[o, at, :].astype(f32)
            velocity = outer_mu * mom[o, at, :].astype(f32) + step_delta
            update = (outer_rate * (step_delta + outer_mu * velocity)).astype(jnp.bfloat16)
            w_v[w_at, :] = (w_v[w_at, :].astype(f32) - update.astype(f32)).astype(jnp.bfloat16)

        here = pl.ds(pl.multiple_of(o * block, block), block)
        copy = pltpu.make_async_copy(w_v.at[here], new_w_hbm.at[here], out_sem.at[1 + d])
        copy.start()
        out_copies.append(copy)

    for copy in hop0 + hop1 + hop2 + mom_copies:
        copy.wait_send()
    for copy in delta_copies[:-1]:
        copy.wait()
    delta_copies[-1].wait()
    for copy in out_copies:
        copy.wait()


def distinct_device(route, inputs, targets, path_weights, momentum):
    n_path = lax.axis_size("path")
    tokens, width = inputs.shape[1:]
    rows, cols = path_weights.shape[1:]
    block = rows // n_path
    chunks = 2
    bf16 = jnp.bfloat16
    held = momentum[:, 0]
    outgoing = select_momentum(route, held)
    any_space = pl.BlockSpec(memory_space=pl.ANY)
    dma = pltpu.SemaphoreType.DMA
    new_weight, received = pl.pallas_call(
        functools.partial(sync_kernel, n_path, chunks),
        out_shape=(
            jax.ShapeDtypeStruct((rows, cols), bf16),
            jax.ShapeDtypeStruct((n_path, block, cols), bf16),
        ),
        in_specs=[any_space] * 4,
        out_specs=(any_space, any_space),
        scratch_shapes=[
            pltpu.VMEM((tokens, width), bf16),
            pltpu.VMEM((tokens, cols), bf16),
            pltpu.VMEM((rows, cols), bf16),
            pltpu.VMEM((tokens, rows), bf16),
            pltpu.VMEM((2 * tokens, rows), bf16),
            pltpu.VMEM((tokens, cols), bf16),
            pltpu.VMEM((tokens, cols), bf16),
            pltpu.VMEM((tokens, cols), jnp.float32),
            pltpu.VMEM((2 * tokens, cols), bf16),
            pltpu.VMEM((n_path, block, cols), bf16),
            pltpu.VMEM((n_path, block, cols), bf16),
            dma((4,)),
            dma((1 + n_path,)),
            dma((3, chunks)),
            dma((3, chunks)),
            dma((n_path - 1,)),
            dma((n_path - 1,)),
            dma((n_path - 1,)),
            dma((n_path - 1,)),
        ],
        compiler_params=pltpu.CompilerParams(
            collective_id=0, has_side_effects=True, vmem_limit_bytes=48 * 2**20
        ),
        cost_estimate=pl.CostEstimate(
            flops=8 * tokens * rows * cols, bytes_accessed=12 * rows * cols, transcendentals=0
        ),
    )(inputs[0], targets[0], path_weights[0], outgoing)
    return (new_weight[None], next_momentum(route, held, received)[:, None])


def solution(mesh):
    placed = (
        P("groups"),
        P(("groups", "path"), "inner", None),
        P(("groups", "path"), "inner", "shard"),
        P(("groups", "path"), "inner", "shard"),
        P("groups", "inner", "path", "shard"),
    )

    def step(route, inputs, targets, path_weights, momentum):
        paths, modules = mesh.shape["path"], momentum.shape[0]
        distinct = 2 <= paths <= modules and mesh.shape["inner"] == 2
        return (distinct_device if distinct else per_device)(route, inputs, targets, path_weights, momentum)

    return jax.shard_map(
        step,
        mesh=mesh,
        in_specs=placed,
        out_specs=(P(("groups", "path"), "inner", "shard"), P("groups", "inner", "path", "shard")),
        check_vma=False,
    )
```

```python
import functools

import jax
import jax.numpy as jnp
from jax import lax
from jax.experimental import pallas as pl
from jax.experimental.pallas import tpu as pltpu
from jax.sharding import PartitionSpec as P

eps = 1e-06
inner_rate = 256.0
outer_rate = 0.7
outer_mu = 0.9


def per_device(route, inputs, targets, path_weights, momentum):
    n_path = lax.axis_size("path")
    tokens = inputs[0]
    target = targets[0]
    weight = path_weights[0]
    width = tokens.shape[1]
    scale = width ** (-0.5)
    xf = tokens.astype(jnp.float32)
    normed = (xf * lax.rsqrt(jnp.mean(xf * xf, axis=-1, keepdims=True) + eps)).astype(jnp.bfloat16)
    normed_cols = lax.all_to_all(normed, "inner", split_axis=1, concat_axis=0, tiled=True)
    tok_path = normed_cols.shape[0]
    coef = inner_rate * scale / tok_path
    output = jnp.dot(
        normed,
        lax.all_gather(weight, "inner", axis=0, tiled=True),
        preferred_element_type=jnp.float32,
    )
    resid = (output * scale - target.astype(jnp.float32)).astype(jnp.bfloat16)
    grad = lax.dot_general(
        normed_cols,
        lax.all_gather(resid, "inner", axis=0, tiled=True),
        (((0,), (0,)), ((), ())),
        preferred_element_type=jnp.float32,
    )
    delta = (grad * coef).astype(jnp.bfloat16)
    blocks = delta.reshape(n_path, weight.shape[0] // n_path, weight.shape[1])
    received = lax.all_to_all(blocks, "path", split_axis=0, concat_axis=0, tiled=True)
    modules = momentum.shape[0]
    onehot = (route[:, None] == jnp.arange(modules, dtype=jnp.int32)[None, :]).astype(jnp.bfloat16)
    counts = jnp.sum(onehot.astype(jnp.float32), axis=0)
    summed = jnp.einsum("pm,prc->mrc", onehot, received, preferred_element_type=jnp.float32)
    mean_delta = summed / jnp.maximum(counts, 1.0)[:, None, None]
    new_velocity = outer_mu * momentum[:, 0] + mean_delta
    update = (outer_rate * (mean_delta + outer_mu * new_velocity)).astype(jnp.bfloat16)
    outgoing = jnp.einsum("pm,mrc->prc", onehot, update, preferred_element_type=jnp.float32).astype(
        jnp.bfloat16
    )
    returned = lax.all_to_all(outgoing, "path", split_axis=0, concat_axis=0, tiled=True)
    returned = returned.reshape(weight.shape[0], weight.shape[1])
    new_weight = (weight.astype(jnp.float32) - returned.astype(jnp.float32)).astype(jnp.bfloat16)
    return (new_weight[None], new_velocity[:, None])


def select_kernel(route_ref, momentum_ref, out_ref, slot_ref, used_ref):
    @pl.when(pl.program_id(0) == 0)
    def _():
        slot = jnp.int32(0)
        for m in range(slot_ref.shape[0]):
            used = jnp.int32(0)
            for p in range(route_ref.shape[0]):
                hit = route_ref[p] == m
                slot = jnp.where(hit, p, slot)
                used = jnp.where(hit, 1, used)
            slot_ref[m] = slot
            used_ref[m] = used

    out_ref[...] = momentum_ref[...].astype(out_ref.dtype)


def select_momentum(route, momentum):
    n_path = route.shape[0]
    modules, rows, cols = momentum.shape
    table = jax.ShapeDtypeStruct((modules,), jnp.int32)
    scalars = pl.BlockSpec(memory_space=pltpu.SMEM)
    return pl.pallas_call(
        select_kernel,
        out_shape=(jax.ShapeDtypeStruct((n_path, rows, cols), jnp.bfloat16), table, table),
        grid_spec=pltpu.PrefetchScalarGridSpec(
            num_scalar_prefetch=1,
            grid=(n_path,),
            in_specs=[pl.BlockSpec((1, rows, cols), lambda p, route: (route[p], 0, 0))],
            out_specs=(pl.BlockSpec((1, rows, cols), lambda p, route: (p, 0, 0)), scalars, scalars),
        ),
        compiler_params=pltpu.CompilerParams(vmem_limit_bytes=57 * 2**20),
        cost_estimate=pl.CostEstimate(flops=0, bytes_accessed=n_path * rows * cols * 6, transcendentals=0),
    )(route, momentum)


def momentum_kernel(slot_ref, used_ref, momentum_ref, delta_ref, weight_ref, out_ref, new_weight_ref, sem):
    m = pl.program_id(0)
    used = used_ref[m]
    handed = pltpu.make_async_copy(weight_ref, new_weight_ref, sem)

    @pl.when(m == 0)
    def _():
        handed.start()

    @pl.when(used != 0)
    def _():
        out_ref[...] = outer_mu * momentum_ref[...] + delta_ref[...].astype(jnp.float32)

    @pl.when(used == 0)
    def _():
        out_ref[...] = outer_mu * momentum_ref[...]

    @pl.when(m == pl.num_programs(0) - 1)
    def _():
        handed.wait()


def next_momentum(slot, used, momentum, received, new_weight):
    modules, rows, cols = momentum.shape
    return pl.pallas_call(
        momentum_kernel,
        out_shape=(
            jax.ShapeDtypeStruct((modules, rows, cols), jnp.float32),
            jax.ShapeDtypeStruct(new_weight.shape, new_weight.dtype),
        ),
        grid_spec=pltpu.PrefetchScalarGridSpec(
            num_scalar_prefetch=2,
            grid=(modules,),
            in_specs=[
                pl.BlockSpec((1, rows, cols), lambda m, slot, used: (m, 0, 0)),
                pl.BlockSpec((1, rows, cols), lambda m, slot, used: (slot[m], 0, 0)),
                pl.BlockSpec(memory_space=pl.ANY),
            ],
            out_specs=(
                pl.BlockSpec((1, rows, cols), lambda m, slot, used: (m, 0, 0)),
                pl.BlockSpec(memory_space=pl.ANY),
            ),
            scratch_shapes=[pltpu.SemaphoreType.DMA],
        ),
        compiler_params=pltpu.CompilerParams(vmem_limit_bytes=57 * 2**20),
        cost_estimate=pl.CostEstimate(flops=0, bytes_accessed=modules * rows * cols * 9, transcendentals=0),
    )(slot, used, momentum, received, new_weight)


def sync_kernel(
    n_path,
    chunks,
    x_hbm,
    t_hbm,
    w_hbm,
    m_hbm,
    new_w_hbm,
    recv_hbm,
    x_v,
    t_v,
    w_v,
    nsend,
    ncols,
    psend,
    precv,
    lp,
    resid,
    delta,
    mom,
    load_sem,
    out_sem,
    x_send,
    x_recv,
    m_send,
    m_recv,
    d_send,
    d_recv,
):
    f32 = jnp.float32
    tokens, width = x_v.shape
    rows, cols = w_v.shape
    block = rows // n_path
    step = tokens // chunks
    tile = min(256, cols)
    scale = width ** (-0.5)
    coef = inner_rate * scale / (2 * tokens)
    me = lax.axis_index("path")
    mine = lax.axis_index("inner")
    other = 1 - mine

    load_x = pltpu.make_async_copy(x_hbm, x_v, load_sem.at[0])
    load_w = pltpu.make_async_copy(w_hbm, w_v, load_sem.at[1])
    load_t = pltpu.make_async_copy(t_hbm, t_v, load_sem.at[2])
    load_m = pltpu.make_async_copy(m_hbm.at[me], mom.at[me], load_sem.at[3])
    load_x.start()
    load_w.start()
    load_t.start()
    load_m.start()

    barrier = pltpu.get_barrier_semaphore()
    pl.semaphore_signal(barrier, inc=1, device_id={"inner": other}, device_id_type=pl.DeviceIdType.MESH)
    for d in range(1, n_path):
        pl.semaphore_signal(
            barrier, inc=1, device_id={"path": lax.rem(me + d, n_path)}, device_id_type=pl.DeviceIdType.MESH
        )
    pl.semaphore_wait(barrier, n_path)

    def far(d, src, dst, send, recv):
        return pltpu.make_async_remote_copy(
            src_ref=src,
            dst_ref=dst,
            send_sem=send.at[d - 1],
            recv_sem=recv.at[d - 1],
            device_id={"path": lax.rem(me + d, n_path)},
            device_id_type=pl.DeviceIdType.MESH,
        )

    def near(hop, c, src, dst):
        return pltpu.make_async_remote_copy(
            src_ref=src,
            dst_ref=dst,
            send_sem=x_send.at[hop, c],
            recv_sem=x_recv.at[hop, c],
            device_id={"inner": other},
            device_id_type=pl.DeviceIdType.MESH,
        )

    mom_copies = [far(d, m_hbm.at[lax.rem(me + d, n_path)], mom.at[me], m_send, m_recv) for d in range(1, n_path)]
    for copy in mom_copies:
        copy.start()

    load_x.wait()
    piece = 32
    own_at = pl.ds(pl.multiple_of(mine * rows, rows), rows)
    other_at = pl.ds(pl.multiple_of(other * rows, rows), rows)
    hop0 = []
    for c in range(chunks):

        @pl.loop(0, step // piece)
        def _(k, c=c):
            at = pl.ds(pl.multiple_of(c * step + k * piece, piece), piece)
            xf = x_v[at, :].astype(f32)
            inv = lax.rsqrt(jnp.mean(xf * xf, axis=-1, keepdims=True) + eps)
            ncols[at, :] = (x_v[at, own_at].astype(f32) * inv).astype(jnp.bfloat16)
            nsend[at, :] = (x_v[at, other_at].astype(f32) * inv).astype(jnp.bfloat16)

        at = pl.ds(c * step, step)
        copy = near(0, c, nsend.at[at], ncols.at[pl.ds(tokens + c * step, step)])
        copy.start()
        hop0.append(copy)

    load_w.wait()
    load_t.wait()

    @pl.loop(0, cols // tile)
    def _(j):
        at = pl.ds(pl.multiple_of(j * tile, tile), tile)
        part = jnp.dot(ncols[0:tokens, :], w_v[:, at], preferred_element_type=f32)
        lp[:, at] = part * scale - t_v[:, at].astype(f32)

    hop1 = []
    for c in range(chunks):
        hop0[c].wait_recv()

        @pl.loop(0, cols // tile)
        def _(j, c=c):
            at = pl.ds(pl.multiple_of(j * tile, tile), tile)
            part = jnp.dot(
                ncols[tokens + c * step : tokens + (c + 1) * step, :], w_v[:, at], preferred_element_type=f32
            )
            psend[c * step : (c + 1) * step, at] = (part * scale).astype(jnp.bfloat16)

        at = pl.ds(c * step, step)
        copy = near(1, c, psend.at[at], precv.at[at])
        copy.start()
        hop1.append(copy)

    hop2 = []
    for c in range(chunks):
        hop1[c].wait_recv()

        @pl.loop(0, step // piece)
        def _(k, c=c):
            at = pl.ds(pl.multiple_of(c * step + k * piece, piece), piece)
            resid[at, :] = (lp[at, :] + precv[at, :].astype(f32)).astype(jnp.bfloat16)

        copy = near(2, c, resid.at[pl.ds(c * step, step)], resid.at[pl.ds(tokens + c * step, step)])
        copy.start()
        hop2.append(copy)
    for copy in hop2:
        copy.wait_recv()

    delta_copies = []
    for d in list(range(1, n_path)) + [0]:
        q = lax.rem(me + d, n_path)
        left = pl.ds(pl.multiple_of(q * block, block), block)

        @pl.loop(0, cols // tile)
        def _(j, q=q, left=left):
            at = pl.ds(pl.multiple_of(j * tile, tile), tile)
            grad = lax.dot_general(
                ncols[:, left], resid[:, at], (((0,), (0,)), ((), ())), preferred_element_type=f32
            )
            delta[q, :, at] = (grad * coef).astype(jnp.bfloat16)

        if d > 0:
            copy = far(d, delta.at[q], recv_hbm.at[me], d_send, d_recv)
        else:
            copy = pltpu.make_async_copy(delta.at[q], recv_hbm.at[me], out_sem.at[0])
        copy.start()
        delta_copies.append(copy)

    out_copies = []
    for d in range(n_path):
        if d == 0:
            load_m.wait()
        else:
            mom_copies[d - 1].wait_recv()
        o = lax.rem(me + n_path - d, n_path)

        @pl.loop(0, block // piece)
        def _(k, o=o):
            at = pl.ds(pl.multiple_of(k * piece, piece), piece)
            w_at = pl.ds(pl.multiple_of(o * block + k * piece, piece), piece)
            step_delta = delta[o, at, :].astype(f32)
            velocity = outer_mu * mom[o, at, :].astype(f32) + step_delta
            update = (outer_rate * (step_delta + outer_mu * velocity)).astype(jnp.bfloat16)
            w_v[w_at, :] = (w_v[w_at, :].astype(f32) - update.astype(f32)).astype(jnp.bfloat16)

        here = pl.ds(pl.multiple_of(o * block, block), block)
        copy = pltpu.make_async_copy(w_v.at[here], new_w_hbm.at[here], out_sem.at[1 + d])
        copy.start()
        out_copies.append(copy)

    for copy in hop0 + hop1 + hop2 + mom_copies:
        copy.wait_send()
    for copy in delta_copies[:-1]:
        copy.wait()
    delta_copies[-1].wait()
    for copy in out_copies:
        copy.wait()


def distinct_device(route, inputs, targets, path_weights, momentum):
    n_path = lax.axis_size("path")
    tokens, width = inputs.shape[1:]
    rows, cols = path_weights.shape[1:]
    block = rows // n_path
    chunks = 2
    bf16 = jnp.bfloat16
    held = momentum[:, 0]
    outgoing, slot, used = select_momentum(route, held)
    any_space = pl.BlockSpec(memory_space=pl.ANY)
    dma = pltpu.SemaphoreType.DMA
    new_weight, received = pl.pallas_call(
        functools.partial(sync_kernel, n_path, chunks),
        out_shape=(
            jax.ShapeDtypeStruct((rows, cols), bf16),
            jax.ShapeDtypeStruct((n_path, block, cols), bf16),
        ),
        in_specs=[pl.BlockSpec(memory_space=pltpu.HBM)] * 3 + [any_space],
        out_specs=(any_space, any_space),
        scratch_shapes=[
            pltpu.VMEM((tokens, width), bf16),
            pltpu.VMEM((tokens, cols), bf16),
            pltpu.VMEM((rows, cols), bf16),
            pltpu.VMEM((tokens, rows), bf16),
            pltpu.VMEM((2 * tokens, rows), bf16),
            pltpu.VMEM((tokens, cols), bf16),
            pltpu.VMEM((tokens, cols), bf16),
            pltpu.VMEM((tokens, cols), jnp.float32),
            pltpu.VMEM((2 * tokens, cols), bf16),
            pltpu.VMEM((n_path, block, cols), bf16),
            pltpu.VMEM((n_path, block, cols), bf16),
            dma((4,)),
            dma((1 + n_path,)),
            dma((3, chunks)),
            dma((3, chunks)),
            dma((n_path - 1,)),
            dma((n_path - 1,)),
            dma((n_path - 1,)),
            dma((n_path - 1,)),
        ],
        compiler_params=pltpu.CompilerParams(
            collective_id=0, has_side_effects=True, vmem_limit_bytes=48 * 2**20
        ),
        cost_estimate=pl.CostEstimate(
            flops=8 * tokens * rows * cols, bytes_accessed=12 * rows * cols, transcendentals=0
        ),
    )(inputs[0], targets[0], path_weights[0], outgoing)
    velocity, new_weight = next_momentum(slot, used, held, received, new_weight)
    return (new_weight[None], velocity[:, None])


def solution(mesh):
    placed = (
        P("groups"),
        P(("groups", "path"), "inner", None),
        P(("groups", "path"), "inner", "shard"),
        P(("groups", "path"), "inner", "shard"),
        P("groups", "inner", "path", "shard"),
    )

    def step(route, inputs, targets, path_weights, momentum):
        paths, modules = mesh.shape["path"], momentum.shape[0]
        distinct = 2 <= paths <= modules and mesh.shape["inner"] == 2
        return (distinct_device if distinct else per_device)(route, inputs, targets, path_weights, momentum)

    return jax.shard_map(
        step,
        mesh=mesh,
        in_specs=placed,
        out_specs=(P(("groups", "path"), "inner", "shard"), P("groups", "inner", "path", "shard")),
        check_vma=False,
    )
```

```python
import functools

import jax
import jax.numpy as jnp
from jax import lax
from jax.experimental import pallas as pl
from jax.experimental.pallas import tpu as pltpu
from jax.sharding import PartitionSpec as P

eps = 1e-06
inner_rate = 256.0
outer_rate = 0.7
outer_mu = 0.9


def per_device(route, inputs, targets, path_weights, momentum):
    n_path = lax.axis_size("path")
    tokens = inputs[0]
    target = targets[0]
    weight = path_weights[0]
    width = tokens.shape[1]
    scale = width ** (-0.5)
    xf = tokens.astype(jnp.float32)
    normed = (xf * lax.rsqrt(jnp.mean(xf * xf, axis=-1, keepdims=True) + eps)).astype(jnp.bfloat16)
    normed_cols = lax.all_to_all(normed, "inner", split_axis=1, concat_axis=0, tiled=True)
    tok_path = normed_cols.shape[0]
    coef = inner_rate * scale / tok_path
    output = jnp.dot(
        normed,
        lax.all_gather(weight, "inner", axis=0, tiled=True),
        preferred_element_type=jnp.float32,
    )
    resid = (output * scale - target.astype(jnp.float32)).astype(jnp.bfloat16)
    grad = lax.dot_general(
        normed_cols,
        lax.all_gather(resid, "inner", axis=0, tiled=True),
        (((0,), (0,)), ((), ())),
        preferred_element_type=jnp.float32,
    )
    delta = (grad * coef).astype(jnp.bfloat16)
    blocks = delta.reshape(n_path, weight.shape[0] // n_path, weight.shape[1])
    received = lax.all_to_all(blocks, "path", split_axis=0, concat_axis=0, tiled=True)
    modules = momentum.shape[0]
    onehot = (route[:, None] == jnp.arange(modules, dtype=jnp.int32)[None, :]).astype(jnp.bfloat16)
    counts = jnp.sum(onehot.astype(jnp.float32), axis=0)
    summed = jnp.einsum("pm,prc->mrc", onehot, received, preferred_element_type=jnp.float32)
    mean_delta = summed / jnp.maximum(counts, 1.0)[:, None, None]
    new_velocity = outer_mu * momentum[:, 0] + mean_delta
    update = (outer_rate * (mean_delta + outer_mu * new_velocity)).astype(jnp.bfloat16)
    outgoing = jnp.einsum("pm,mrc->prc", onehot, update, preferred_element_type=jnp.float32).astype(
        jnp.bfloat16
    )
    returned = lax.all_to_all(outgoing, "path", split_axis=0, concat_axis=0, tiled=True)
    returned = returned.reshape(weight.shape[0], weight.shape[1])
    new_weight = (weight.astype(jnp.float32) - returned.astype(jnp.float32)).astype(jnp.bfloat16)
    return (new_weight[None], new_velocity[:, None])


def path_of(route_ref, m):
    slot, used = jnp.int32(0), jnp.int32(0)
    for p in range(route_ref.shape[0]):
        hit = route_ref[p] == m
        slot = jnp.where(hit, p, slot)
        used = jnp.where(hit, 1, used)
    return slot, used


def momentum_kernel(route_ref, momentum_ref, delta_ref, out_ref):
    _, used = path_of(route_ref, pl.program_id(0))

    @pl.when(used != 0)
    def _():
        out_ref[...] = outer_mu * momentum_ref[...] + delta_ref[...].astype(jnp.float32)

    @pl.when(used == 0)
    def _():
        out_ref[...] = outer_mu * momentum_ref[...]


def next_momentum(route, momentum, received):
    modules, rows, cols = momentum.shape
    return pl.pallas_call(
        momentum_kernel,
        out_shape=jax.ShapeDtypeStruct((modules, rows, cols), jnp.float32),
        grid_spec=pltpu.PrefetchScalarGridSpec(
            num_scalar_prefetch=1,
            grid=(modules,),
            in_specs=[
                pl.BlockSpec((1, rows, cols), lambda m, route: (m, 0, 0)),
                pl.BlockSpec((1, rows, cols), lambda m, route: (path_of(route, m)[0], 0, 0)),
            ],
            out_specs=pl.BlockSpec((1, rows, cols), lambda m, route: (m, 0, 0)),
        ),
        compiler_params=pltpu.CompilerParams(vmem_limit_bytes=32 * 2**20),
        cost_estimate=pl.CostEstimate(flops=0, bytes_accessed=modules * rows * cols * 9, transcendentals=0),
    )(route, momentum, received)


def sync_kernel(
    n_path,
    chunks,
    route_ref,
    x_hbm,
    t_hbm,
    w_hbm,
    m_hbm,
    new_w_hbm,
    recv_hbm,
    held_hbm,
    x_v,
    t_v,
    w_v,
    nsend,
    ncols,
    psend,
    precv,
    lp,
    resid,
    delta,
    mom,
    held,
    msend,
    load_sem,
    held_sem,
    out_sem,
    x_send,
    x_recv,
    m_send,
    m_recv,
    d_send,
    d_recv,
):
    f32 = jnp.float32
    tokens, width = x_v.shape
    rows, cols = w_v.shape
    block = rows // n_path
    step = tokens // chunks
    tile = min(256, cols)
    scale = width ** (-0.5)
    coef = inner_rate * scale / (2 * tokens)
    me = lax.axis_index("path")
    mine = lax.axis_index("inner")
    other = 1 - mine

    load_x = pltpu.make_async_copy(x_hbm, x_v, load_sem.at[0])
    load_w = pltpu.make_async_copy(w_hbm, w_v, load_sem.at[1])
    load_t = pltpu.make_async_copy(t_hbm, t_v, load_sem.at[2])
    load_m = pltpu.make_async_copy(msend.at[me], mom.at[me], load_sem.at[3])
    cuts = held_sem.shape[0] // 2
    strip = block // cuts
    strips = [pl.ds(c * strip, strip) for c in range(cuts)]
    take = [pltpu.make_async_copy(m_hbm.at[:, at], held.at[:, at], held_sem.at[c]) for c, at in enumerate(strips)]
    give = [
        pltpu.make_async_copy(held.at[:, at], held_hbm.at[:, at], held_sem.at[cuts + c]) for c, at in enumerate(strips)
    ]
    take[0].start()
    load_x.start()
    for copy in take[1:]:
        copy.start()
    load_w.start()
    load_t.start()

    barrier = pltpu.get_barrier_semaphore()
    pl.semaphore_signal(barrier, inc=1, device_id={"inner": other}, device_id_type=pl.DeviceIdType.MESH)
    for d in range(1, n_path):
        pl.semaphore_signal(
            barrier, inc=1, device_id={"path": lax.rem(me + d, n_path)}, device_id_type=pl.DeviceIdType.MESH
        )
    pl.semaphore_wait(barrier, n_path)

    def far(d, src, dst, send, recv, c=0):
        return pltpu.make_async_remote_copy(
            src_ref=src,
            dst_ref=dst,
            send_sem=send.at[c, d - 1],
            recv_sem=recv.at[c, d - 1],
            device_id={"path": lax.rem(me + d, n_path)},
            device_id_type=pl.DeviceIdType.MESH,
        )

    def near(hop, c, src, dst):
        return pltpu.make_async_remote_copy(
            src_ref=src,
            dst_ref=dst,
            send_sem=x_send.at[hop, c],
            recv_sem=x_recv.at[hop, c],
            device_id={"inner": other},
            device_id_type=pl.DeviceIdType.MESH,
        )

    modules = held.shape[0]
    mom_copies = []
    for c, at in enumerate(strips):
        take[c].wait()

        @pl.loop(0, strip // 16)
        def _(k, c=c):
            rows_at = pl.ds(pl.multiple_of(c * strip + k * 16, 16), 16)
            for p in range(n_path):
                chosen = held[0, rows_at, :]
                for m in range(1, modules):
                    chosen = jnp.where(route_ref[p] == m, held[m, rows_at, :], chosen)
                msend[p, rows_at, :] = chosen.astype(jnp.bfloat16)

        for d in range(1, n_path):
            copy = far(d, msend.at[lax.rem(me + d, n_path), at], mom.at[me, at], m_send, m_recv, c)
            copy.start()
            mom_copies.append((d, copy))
        give[c].start()
    load_m.start()

    load_x.wait()
    piece = 32
    own_at = pl.ds(pl.multiple_of(mine * rows, rows), rows)
    other_at = pl.ds(pl.multiple_of(other * rows, rows), rows)
    hop0 = []
    for c in range(chunks):

        @pl.loop(0, step // piece)
        def _(k, c=c):
            at = pl.ds(pl.multiple_of(c * step + k * piece, piece), piece)
            xf = x_v[at, :].astype(f32)
            inv = lax.rsqrt(jnp.mean(xf * xf, axis=-1, keepdims=True) + eps)
            ncols[at, :] = (x_v[at, own_at].astype(f32) * inv).astype(jnp.bfloat16)
            nsend[at, :] = (x_v[at, other_at].astype(f32) * inv).astype(jnp.bfloat16)

        at = pl.ds(c * step, step)
        copy = near(0, c, nsend.at[at], ncols.at[pl.ds(tokens + c * step, step)])
        copy.start()
        hop0.append(copy)

    load_w.wait()
    load_t.wait()

    @pl.loop(0, cols // tile)
    def _(j):
        at = pl.ds(pl.multiple_of(j * tile, tile), tile)
        part = jnp.dot(ncols[0:tokens, :], w_v[:, at], preferred_element_type=f32)
        lp[:, at] = part * scale - t_v[:, at].astype(f32)

    hop1 = []
    for c in range(chunks):
        hop0[c].wait_recv()

        @pl.loop(0, cols // tile)
        def _(j, c=c):
            at = pl.ds(pl.multiple_of(j * tile, tile), tile)
            part = jnp.dot(
                ncols[tokens + c * step : tokens + (c + 1) * step, :], w_v[:, at], preferred_element_type=f32
            )
            psend[c * step : (c + 1) * step, at] = (part * scale).astype(jnp.bfloat16)

        at = pl.ds(c * step, step)
        copy = near(1, c, psend.at[at], precv.at[at])
        copy.start()
        hop1.append(copy)

    hop2 = []
    for c in range(chunks):
        hop1[c].wait_recv()

        @pl.loop(0, step // piece)
        def _(k, c=c):
            at = pl.ds(pl.multiple_of(c * step + k * piece, piece), piece)
            resid[at, :] = (lp[at, :] + precv[at, :].astype(f32)).astype(jnp.bfloat16)

        copy = near(2, c, resid.at[pl.ds(c * step, step)], resid.at[pl.ds(tokens + c * step, step)])
        copy.start()
        hop2.append(copy)
    for copy in hop2:
        copy.wait_recv()

    delta_copies = []
    for d in list(range(1, n_path)) + [0]:
        q = lax.rem(me + d, n_path)
        left = pl.ds(pl.multiple_of(q * block, block), block)

        @pl.loop(0, cols // tile)
        def _(j, q=q, left=left):
            at = pl.ds(pl.multiple_of(j * tile, tile), tile)
            grad = lax.dot_general(
                ncols[:, left], resid[:, at], (((0,), (0,)), ((), ())), preferred_element_type=f32
            )
            delta[q, :, at] = (grad * coef).astype(jnp.bfloat16)

        if d > 0:
            copy = far(d, delta.at[q], recv_hbm.at[me], d_send, d_recv)
        else:
            copy = pltpu.make_async_copy(delta.at[q], recv_hbm.at[me], out_sem.at[0])
        copy.start()
        delta_copies.append(copy)

    out_copies = []
    for d in range(n_path):
        if d == 0:
            load_m.wait()
        else:
            for offset, copy in mom_copies:
                if offset == d:
                    copy.wait_recv()
        o = lax.rem(me + n_path - d, n_path)

        @pl.loop(0, block // piece)
        def _(k, o=o):
            at = pl.ds(pl.multiple_of(k * piece, piece), piece)
            w_at = pl.ds(pl.multiple_of(o * block + k * piece, piece), piece)
            step_delta = delta[o, at, :].astype(f32)
            velocity = outer_mu * mom[o, at, :].astype(f32) + step_delta
            update = (outer_rate * (step_delta + outer_mu * velocity)).astype(jnp.bfloat16)
            w_v[w_at, :] = (w_v[w_at, :].astype(f32) - update.astype(f32)).astype(jnp.bfloat16)

        here = pl.ds(pl.multiple_of(o * block, block), block)
        copy = pltpu.make_async_copy(w_v.at[here], new_w_hbm.at[here], out_sem.at[1 + d])
        copy.start()
        out_copies.append(copy)

    for copy in hop0 + hop1 + hop2 + [copy for _, copy in mom_copies]:
        copy.wait_send()
    for copy in give:
        copy.wait()
    for copy in delta_copies[:-1]:
        copy.wait()
    delta_copies[-1].wait()
    for copy in out_copies:
        copy.wait()


def distinct_device(route, inputs, targets, path_weights, momentum):
    n_path = lax.axis_size("path")
    tokens, width = inputs.shape[1:]
    rows, cols = path_weights.shape[1:]
    block = rows // n_path
    chunks = 2
    bf16 = jnp.bfloat16
    held = momentum[:, 0]
    cuts = 4
    any_space = pl.BlockSpec(memory_space=pl.ANY)
    dma = pltpu.SemaphoreType.DMA
    new_weight, received, kept = pl.pallas_call(
        functools.partial(sync_kernel, n_path, chunks),
        out_shape=(
            jax.ShapeDtypeStruct((rows, cols), bf16),
            jax.ShapeDtypeStruct((n_path, block, cols), bf16),
            jax.ShapeDtypeStruct(held.shape, held.dtype),
        ),
        in_specs=[pl.BlockSpec(memory_space=pltpu.SMEM)] + [any_space] * 4,
        out_specs=(any_space,) * 3,
        scratch_shapes=[
            pltpu.VMEM((tokens, width), bf16),
            pltpu.VMEM((tokens, cols), bf16),
            pltpu.VMEM((rows, cols), bf16),
            pltpu.VMEM((tokens, rows), bf16),
            pltpu.VMEM((2 * tokens, rows), bf16),
            pltpu.VMEM((tokens, cols), bf16),
            pltpu.VMEM((tokens, cols), bf16),
            pltpu.VMEM((tokens, cols), jnp.float32),
            pltpu.VMEM((2 * tokens, cols), bf16),
            pltpu.VMEM((n_path, block, cols), bf16),
            pltpu.VMEM((n_path, block, cols), bf16),
            pltpu.VMEM(held.shape, held.dtype),
            pltpu.VMEM((n_path, block, cols), bf16),
            dma((4,)),
            dma((2 * cuts,)),
            dma((1 + n_path,)),
            dma((3, chunks)),
            dma((3, chunks)),
            dma((cuts, n_path - 1)),
            dma((cuts, n_path - 1)),
            dma((1, n_path - 1)),
            dma((1, n_path - 1)),
        ],
        compiler_params=pltpu.CompilerParams(
            collective_id=0, has_side_effects=True, vmem_limit_bytes=38 * 2**20
        ),
        cost_estimate=pl.CostEstimate(
            flops=8 * tokens * rows * cols, bytes_accessed=12 * rows * cols, transcendentals=0
        ),
    )(route, *[pltpu.with_memory_space_constraint(a, pltpu.HBM) for a in (inputs[0], targets[0], path_weights[0], held)])
    return (new_weight[None], next_momentum(route, kept, received)[:, None])


def solution(mesh):
    placed = (
        P("groups"),
        P(("groups", "path"), "inner", None),
        P(("groups", "path"), "inner", "shard"),
        P(("groups", "path"), "inner", "shard"),
        P("groups", "inner", "path", "shard"),
    )

    def step(route, inputs, targets, path_weights, momentum):
        paths, modules = mesh.shape["path"], momentum.shape[0]
        distinct = 2 <= paths <= modules and mesh.shape["inner"] == 2
        return (distinct_device if distinct else per_device)(route, inputs, targets, path_weights, momentum)

    return jax.shard_map(
        step,
        mesh=mesh,
        in_specs=placed,
        out_specs=(P(("groups", "path"), "inner", "shard"), P("groups", "inner", "path", "shard")),
        check_vma=False,
    )
```

```python
import functools

import jax
import jax.numpy as jnp
from jax import lax
from jax.experimental import pallas as pl
from jax.experimental.pallas import tpu as pltpu
from jax.sharding import PartitionSpec as P

eps = 1e-06
inner_rate = 256.0
outer_rate = 0.7
outer_mu = 0.9


def per_device(route, inputs, targets, path_weights, momentum):
    n_path = lax.axis_size("path")
    tokens = inputs[0]
    target = targets[0]
    weight = path_weights[0]
    width = tokens.shape[1]
    scale = width ** (-0.5)
    xf = tokens.astype(jnp.float32)
    normed = (xf * lax.rsqrt(jnp.mean(xf * xf, axis=-1, keepdims=True) + eps)).astype(jnp.bfloat16)
    normed_cols = lax.all_to_all(normed, "inner", split_axis=1, concat_axis=0, tiled=True)
    tok_path = normed_cols.shape[0]
    coef = inner_rate * scale / tok_path
    output = jnp.dot(
        normed,
        lax.all_gather(weight, "inner", axis=0, tiled=True),
        preferred_element_type=jnp.float32,
    )
    resid = (output * scale - target.astype(jnp.float32)).astype(jnp.bfloat16)
    grad = lax.dot_general(
        normed_cols,
        lax.all_gather(resid, "inner", axis=0, tiled=True),
        (((0,), (0,)), ((), ())),
        preferred_element_type=jnp.float32,
    )
    delta = (grad * coef).astype(jnp.bfloat16)
    blocks = delta.reshape(n_path, weight.shape[0] // n_path, weight.shape[1])
    received = lax.all_to_all(blocks, "path", split_axis=0, concat_axis=0, tiled=True)
    modules = momentum.shape[0]
    onehot = (route[:, None] == jnp.arange(modules, dtype=jnp.int32)[None, :]).astype(jnp.bfloat16)
    counts = jnp.sum(onehot.astype(jnp.float32), axis=0)
    summed = jnp.einsum("pm,prc->mrc", onehot, received, preferred_element_type=jnp.float32)
    mean_delta = summed / jnp.maximum(counts, 1.0)[:, None, None]
    new_velocity = outer_mu * momentum[:, 0] + mean_delta
    update = (outer_rate * (mean_delta + outer_mu * new_velocity)).astype(jnp.bfloat16)
    outgoing = jnp.einsum("pm,mrc->prc", onehot, update, preferred_element_type=jnp.float32).astype(
        jnp.bfloat16
    )
    returned = lax.all_to_all(outgoing, "path", split_axis=0, concat_axis=0, tiled=True)
    returned = returned.reshape(weight.shape[0], weight.shape[1])
    new_weight = (weight.astype(jnp.float32) - returned.astype(jnp.float32)).astype(jnp.bfloat16)
    return (new_weight[None], new_velocity[:, None])


def momentum_kernel(route_ref, decayed_ref, delta_ref, weight_ref, out_ref, new_weight_ref):
    out_ref[...] = decayed_ref[...] + delta_ref[...].astype(jnp.float32)


def next_momentum(route, decayed, received, new_weight):
    modules, rows, cols = decayed.shape
    n_path = received.shape[0]
    module = pl.BlockSpec((1, rows, cols), lambda p, route: (route[p], 0, 0))
    whole = pl.BlockSpec(memory_space=pl.ANY)
    return pl.pallas_call(
        momentum_kernel,
        out_shape=(
            jax.ShapeDtypeStruct((modules, rows, cols), jnp.float32),
            jax.ShapeDtypeStruct(new_weight.shape, new_weight.dtype),
        ),
        grid_spec=pltpu.PrefetchScalarGridSpec(
            num_scalar_prefetch=1,
            grid=(n_path,),
            in_specs=[module, pl.BlockSpec((1, rows, cols), lambda p, route: (p, 0, 0)), whole],
            out_specs=(module, whole),
        ),
        input_output_aliases={1: 0, 3: 1},
        compiler_params=pltpu.CompilerParams(vmem_limit_bytes=32 * 2**20),
        cost_estimate=pl.CostEstimate(flops=0, bytes_accessed=n_path * rows * cols * 10, transcendentals=0),
    )(route, decayed, received, new_weight)


def sync_kernel(
    n_path,
    chunks,
    route_ref,
    x_hbm,
    t_hbm,
    w_hbm,
    m_hbm,
    new_w_hbm,
    recv_hbm,
    held_hbm,
    x_v,
    t_v,
    w_v,
    nsend,
    ncols,
    psend,
    precv,
    lp,
    resid,
    delta,
    mom,
    held,
    msend,
    load_sem,
    held_sem,
    out_sem,
    x_send,
    x_recv,
    m_send,
    m_recv,
    d_send,
    d_recv,
):
    f32 = jnp.float32
    tokens, width = x_v.shape
    rows, cols = w_v.shape
    block = rows // n_path
    step = tokens // chunks
    tile = min(256, cols)
    scale = width ** (-0.5)
    coef = inner_rate * scale / (2 * tokens)
    me = lax.axis_index("path")
    mine = lax.axis_index("inner")
    other = 1 - mine

    load_x = pltpu.make_async_copy(x_hbm, x_v, load_sem.at[0])
    load_w = pltpu.make_async_copy(w_hbm, w_v, load_sem.at[1])
    load_t = pltpu.make_async_copy(t_hbm, t_v, load_sem.at[2])
    load_m = pltpu.make_async_copy(msend.at[me], mom.at[me], load_sem.at[3])
    cuts = held_sem.shape[0] // 2
    strip = block // cuts
    strips = [pl.ds(c * strip, strip) for c in range(cuts)]
    take = [pltpu.make_async_copy(m_hbm.at[:, at], held.at[:, at], held_sem.at[c]) for c, at in enumerate(strips)]
    give = [
        pltpu.make_async_copy(held.at[:, at], held_hbm.at[:, at], held_sem.at[cuts + c]) for c, at in enumerate(strips)
    ]
    take[0].start()
    load_x.start()
    for copy in take[1:]:
        copy.start()
    load_w.start()
    load_t.start()

    barrier = pltpu.get_barrier_semaphore()
    pl.semaphore_signal(barrier, inc=1, device_id={"inner": other}, device_id_type=pl.DeviceIdType.MESH)
    for d in range(1, n_path):
        pl.semaphore_signal(
            barrier, inc=1, device_id={"path": lax.rem(me + d, n_path)}, device_id_type=pl.DeviceIdType.MESH
        )
    pl.semaphore_wait(barrier, n_path)

    def far(d, src, dst, send, recv, c=0):
        return pltpu.make_async_remote_copy(
            src_ref=src,
            dst_ref=dst,
            send_sem=send.at[c, d - 1],
            recv_sem=recv.at[c, d - 1],
            device_id={"path": lax.rem(me + d, n_path)},
            device_id_type=pl.DeviceIdType.MESH,
        )

    def near(hop, c, src, dst):
        return pltpu.make_async_remote_copy(
            src_ref=src,
            dst_ref=dst,
            send_sem=x_send.at[hop, c],
            recv_sem=x_recv.at[hop, c],
            device_id={"inner": other},
            device_id_type=pl.DeviceIdType.MESH,
        )

    modules = held.shape[0]
    mom_copies = []
    for c, at in enumerate(strips):
        take[c].wait()

        @pl.loop(0, strip // 16)
        def _(k, c=c):
            rows_at = pl.ds(pl.multiple_of(c * strip + k * 16, 16), 16)
            for p in range(n_path):
                chosen = held[0, rows_at, :]
                for m in range(1, modules):
                    chosen = jnp.where(route_ref[p] == m, held[m, rows_at, :], chosen)
                msend[p, rows_at, :] = chosen.astype(jnp.bfloat16)
            held[:, rows_at, :] = outer_mu * held[:, rows_at, :]

        for d in range(1, n_path):
            copy = far(d, msend.at[lax.rem(me + d, n_path), at], mom.at[me, at], m_send, m_recv, c)
            copy.start()
            mom_copies.append((d, copy))
        give[c].start()
    load_m.start()

    load_x.wait()
    piece = 32
    own_at = pl.ds(pl.multiple_of(mine * rows, rows), rows)
    other_at = pl.ds(pl.multiple_of(other * rows, rows), rows)
    hop0 = []
    for c in range(chunks):

        @pl.loop(0, step // piece)
        def _(k, c=c):
            at = pl.ds(pl.multiple_of(c * step + k * piece, piece), piece)
            xf = x_v[at, :].astype(f32)
            inv = lax.rsqrt(jnp.mean(xf * xf, axis=-1, keepdims=True) + eps)
            ncols[at, :] = (x_v[at, own_at].astype(f32) * inv).astype(jnp.bfloat16)
            nsend[at, :] = (x_v[at, other_at].astype(f32) * inv).astype(jnp.bfloat16)

        at = pl.ds(c * step, step)
        copy = near(0, c, nsend.at[at], ncols.at[pl.ds(tokens + c * step, step)])
        copy.start()
        hop0.append(copy)

    load_w.wait()
    load_t.wait()

    @pl.loop(0, cols // tile)
    def _(j):
        at = pl.ds(pl.multiple_of(j * tile, tile), tile)
        part = jnp.dot(ncols[0:tokens, :], w_v[:, at], preferred_element_type=f32)
        lp[:, at] = part * scale - t_v[:, at].astype(f32)

    hop1 = []
    for c in range(chunks):
        hop0[c].wait_recv()

        @pl.loop(0, cols // tile)
        def _(j, c=c):
            at = pl.ds(pl.multiple_of(j * tile, tile), tile)
            part = jnp.dot(
                ncols[tokens + c * step : tokens + (c + 1) * step, :], w_v[:, at], preferred_element_type=f32
            )
            psend[c * step : (c + 1) * step, at] = (part * scale).astype(jnp.bfloat16)

        at = pl.ds(c * step, step)
        copy = near(1, c, psend.at[at], precv.at[at])
        copy.start()
        hop1.append(copy)

    hop2 = []
    for c in range(chunks):
        hop1[c].wait_recv()

        @pl.loop(0, step // piece)
        def _(k, c=c):
            at = pl.ds(pl.multiple_of(c * step + k * piece, piece), piece)
            resid[at, :] = (lp[at, :] + precv[at, :].astype(f32)).astype(jnp.bfloat16)

        copy = near(2, c, resid.at[pl.ds(c * step, step)], resid.at[pl.ds(tokens + c * step, step)])
        copy.start()
        hop2.append(copy)
    for copy in hop2:
        copy.wait_recv()

    delta_copies = []
    for d in list(range(1, n_path)) + [0]:
        q = lax.rem(me + d, n_path)
        left = pl.ds(pl.multiple_of(q * block, block), block)

        @pl.loop(0, cols // tile)
        def _(j, q=q, left=left):
            at = pl.ds(pl.multiple_of(j * tile, tile), tile)
            grad = lax.dot_general(
                ncols[:, left], resid[:, at], (((0,), (0,)), ((), ())), preferred_element_type=f32
            )
            delta[q, :, at] = (grad * coef).astype(jnp.bfloat16)

        if d > 0:
            copy = far(d, delta.at[q], recv_hbm.at[me], d_send, d_recv)
        else:
            copy = pltpu.make_async_copy(delta.at[q], recv_hbm.at[me], out_sem.at[0])
        copy.start()
        delta_copies.append(copy)

    out_copies = []
    for d in range(n_path):
        if d == 0:
            load_m.wait()
        else:
            for offset, copy in mom_copies:
                if offset == d:
                    copy.wait_recv()
        o = lax.rem(me + n_path - d, n_path)

        @pl.loop(0, block // piece)
        def _(k, o=o):
            at = pl.ds(pl.multiple_of(k * piece, piece), piece)
            w_at = pl.ds(pl.multiple_of(o * block + k * piece, piece), piece)
            step_delta = delta[o, at, :].astype(f32)
            velocity = outer_mu * mom[o, at, :].astype(f32) + step_delta
            update = (outer_rate * (step_delta + outer_mu * velocity)).astype(jnp.bfloat16)
            w_v[w_at, :] = (w_v[w_at, :].astype(f32) - update.astype(f32)).astype(jnp.bfloat16)

        here = pl.ds(pl.multiple_of(o * block, block), block)
        copy = pltpu.make_async_copy(w_v.at[here], new_w_hbm.at[here], out_sem.at[1 + d])
        copy.start()
        out_copies.append(copy)

    for copy in hop0 + hop1 + hop2 + [copy for _, copy in mom_copies]:
        copy.wait_send()
    for copy in give:
        copy.wait()
    for copy in delta_copies[:-1]:
        copy.wait()
    delta_copies[-1].wait()
    for copy in out_copies:
        copy.wait()


def distinct_device(route, inputs, targets, path_weights, momentum):
    n_path = lax.axis_size("path")
    tokens, width = inputs.shape[1:]
    rows, cols = path_weights.shape[1:]
    block = rows // n_path
    chunks = 2
    bf16 = jnp.bfloat16
    held = momentum[:, 0]
    route = pltpu.with_memory_space_constraint(route, pltpu.HBM)
    cuts = 4
    any_space = pl.BlockSpec(memory_space=pl.ANY)
    dma = pltpu.SemaphoreType.DMA
    new_weight, received, kept = pl.pallas_call(
        functools.partial(sync_kernel, n_path, chunks),
        out_shape=(
            jax.ShapeDtypeStruct((rows, cols), bf16),
            jax.ShapeDtypeStruct((n_path, block, cols), bf16),
            jax.ShapeDtypeStruct(held.shape, held.dtype),
        ),
        in_specs=[pl.BlockSpec(memory_space=pltpu.SMEM)] + [any_space] * 4,
        out_specs=(any_space,) * 3,
        scratch_shapes=[
            pltpu.VMEM((tokens, width), bf16),
            pltpu.VMEM((tokens, cols), bf16),
            pltpu.VMEM((rows, cols), bf16),
            pltpu.VMEM((tokens, rows), bf16),
            pltpu.VMEM((2 * tokens, rows), bf16),
            pltpu.VMEM((tokens, cols), bf16),
            pltpu.VMEM((tokens, cols), bf16),
            pltpu.VMEM((tokens, cols), jnp.float32),
            pltpu.VMEM((2 * tokens, cols), bf16),
            pltpu.VMEM((n_path, block, cols), bf16),
            pltpu.VMEM((n_path, block, cols), bf16),
            pltpu.VMEM(held.shape, held.dtype),
            pltpu.VMEM((n_path, block, cols), bf16),
            dma((4,)),
            dma((2 * cuts,)),
            dma((1 + n_path,)),
            dma((3, chunks)),
            dma((3, chunks)),
            dma((cuts, n_path - 1)),
            dma((cuts, n_path - 1)),
            dma((1, n_path - 1)),
            dma((1, n_path - 1)),
        ],
        compiler_params=pltpu.CompilerParams(
            collective_id=0, has_side_effects=True, vmem_limit_bytes=38 * 2**20
        ),
        cost_estimate=pl.CostEstimate(
            flops=8 * tokens * rows * cols, bytes_accessed=12 * rows * cols, transcendentals=0
        ),
    )(route, *[pltpu.with_memory_space_constraint(a, pltpu.HBM) for a in (inputs[0], targets[0], path_weights[0], held)])
    velocity, new_weight = next_momentum(route, kept, received, new_weight)
    return (new_weight[None], velocity[:, None])


def solution(mesh):
    placed = (
        P("groups"),
        P(("groups", "path"), "inner", None),
        P(("groups", "path"), "inner", "shard"),
        P(("groups", "path"), "inner", "shard"),
        P("groups", "inner", "path", "shard"),
    )

    def step(route, inputs, targets, path_weights, momentum):
        paths, modules = mesh.shape["path"], momentum.shape[0]
        distinct = 2 <= paths <= modules and mesh.shape["inner"] == 2
        return (distinct_device if distinct else per_device)(route, inputs, targets, path_weights, momentum)

    return jax.shard_map(
        step,
        mesh=mesh,
        in_specs=placed,
        out_specs=(P(("groups", "path"), "inner", "shard"), P("groups", "inner", "path", "shard")),
        check_vma=False,
    )
```

```python
import functools

import jax
import jax.numpy as jnp
from jax import lax
from jax.experimental import pallas as pl
from jax.experimental.pallas import tpu as pltpu
from jax.sharding import PartitionSpec as P

eps = 1e-06
inner_rate = 256.0
outer_rate = 0.7
outer_mu = 0.9


def per_device(route, inputs, targets, path_weights, momentum):
    n_path = lax.axis_size("path")
    tokens = inputs[0]
    target = targets[0]
    weight = path_weights[0]
    width = tokens.shape[1]
    scale = width ** (-0.5)
    xf = tokens.astype(jnp.float32)
    normed = (xf * lax.rsqrt(jnp.mean(xf * xf, axis=-1, keepdims=True) + eps)).astype(jnp.bfloat16)
    normed_cols = lax.all_to_all(normed, "inner", split_axis=1, concat_axis=0, tiled=True)
    tok_path = normed_cols.shape[0]
    coef = inner_rate * scale / tok_path
    output = jnp.dot(
        normed,
        lax.all_gather(weight, "inner", axis=0, tiled=True),
        preferred_element_type=jnp.float32,
    )
    resid = (output * scale - target.astype(jnp.float32)).astype(jnp.bfloat16)
    grad = lax.dot_general(
        normed_cols,
        lax.all_gather(resid, "inner", axis=0, tiled=True),
        (((0,), (0,)), ((), ())),
        preferred_element_type=jnp.float32,
    )
    delta = (grad * coef).astype(jnp.bfloat16)
    blocks = delta.reshape(n_path, weight.shape[0] // n_path, weight.shape[1])
    received = lax.all_to_all(blocks, "path", split_axis=0, concat_axis=0, tiled=True)
    modules = momentum.shape[0]
    onehot = (route[:, None] == jnp.arange(modules, dtype=jnp.int32)[None, :]).astype(jnp.bfloat16)
    counts = jnp.sum(onehot.astype(jnp.float32), axis=0)
    summed = jnp.einsum("pm,prc->mrc", onehot, received, preferred_element_type=jnp.float32)
    mean_delta = summed / jnp.maximum(counts, 1.0)[:, None, None]
    new_velocity = outer_mu * momentum[:, 0] + mean_delta
    update = (outer_rate * (mean_delta + outer_mu * new_velocity)).astype(jnp.bfloat16)
    outgoing = jnp.einsum("pm,mrc->prc", onehot, update, preferred_element_type=jnp.float32).astype(
        jnp.bfloat16
    )
    returned = lax.all_to_all(outgoing, "path", split_axis=0, concat_axis=0, tiled=True)
    returned = returned.reshape(weight.shape[0], weight.shape[1])
    new_weight = (weight.astype(jnp.float32) - returned.astype(jnp.float32)).astype(jnp.bfloat16)
    return (new_weight[None], new_velocity[:, None])


def momentum_kernel(route_ref, decayed_ref, delta_ref, weight_ref, out_ref, new_weight_ref):
    out_ref[...] = decayed_ref[...] + delta_ref[...].astype(jnp.float32)


def next_momentum(route, decayed, received, new_weight):
    modules, rows, cols = decayed.shape
    n_path = received.shape[0]
    module = pl.BlockSpec((1, rows, cols), lambda p, route: (route[p], 0, 0))
    whole = pl.BlockSpec(memory_space=pl.ANY)
    return pl.pallas_call(
        momentum_kernel,
        out_shape=(
            jax.ShapeDtypeStruct((modules, rows, cols), jnp.float32),
            jax.ShapeDtypeStruct(new_weight.shape, new_weight.dtype),
        ),
        grid_spec=pltpu.PrefetchScalarGridSpec(
            num_scalar_prefetch=1,
            grid=(n_path,),
            in_specs=[module, pl.BlockSpec((1, rows, cols), lambda p, route: (p, 0, 0)), whole],
            out_specs=(module, whole),
        ),
        input_output_aliases={1: 0, 3: 1},
        compiler_params=pltpu.CompilerParams(vmem_limit_bytes=32 * 2**20),
        cost_estimate=pl.CostEstimate(flops=0, bytes_accessed=n_path * rows * cols * 10, transcendentals=0),
    )(route, decayed, received, new_weight)


def sync_kernel(
    n_path,
    chunks,
    route_ref,
    x_hbm,
    t_hbm,
    w_hbm,
    m_hbm,
    new_w_hbm,
    recv_hbm,
    held_hbm,
    x_v,
    t_v,
    w_v,
    nsend,
    ncols,
    psend,
    precv,
    lp,
    resid,
    delta,
    mom,
    held,
    msend,
    load_sem,
    held_sem,
    out_sem,
    x_send,
    x_recv,
    m_send,
    m_recv,
    d_send,
    d_recv,
):
    f32 = jnp.float32
    tokens, width = x_v.shape
    rows, cols = w_v.shape
    block = rows // n_path
    step = tokens // chunks
    tile = min(256, cols)
    scale = width ** (-0.5)
    coef = inner_rate * scale / (2 * tokens)
    me = lax.axis_index("path")
    mine = lax.axis_index("inner")
    other = 1 - mine

    load_x = pltpu.make_async_copy(x_hbm, x_v, load_sem.at[0])
    load_w = pltpu.make_async_copy(w_hbm, w_v, load_sem.at[1])
    load_t = pltpu.make_async_copy(t_hbm, t_v, load_sem.at[2])
    load_m = pltpu.make_async_copy(msend.at[me], mom.at[me], load_sem.at[3])
    cuts = held_sem.shape[0] // 2
    strip = block // cuts
    strips = [pl.ds(c * strip, strip) for c in range(cuts)]
    take = [pltpu.make_async_copy(m_hbm.at[:, at], held.at[:, at], held_sem.at[c]) for c, at in enumerate(strips)]
    give = [
        pltpu.make_async_copy(held.at[:, at], held_hbm.at[:, at], held_sem.at[cuts + c]) for c, at in enumerate(strips)
    ]
    take[0].start()
    load_x.start()
    for copy in take[1:]:
        copy.start()
    load_w.start()
    load_t.start()

    barrier = pltpu.get_barrier_semaphore()
    pl.semaphore_signal(barrier, inc=1, device_id={"inner": other}, device_id_type=pl.DeviceIdType.MESH)
    for d in range(1, n_path):
        pl.semaphore_signal(
            barrier, inc=1, device_id={"path": lax.rem(me + d, n_path)}, device_id_type=pl.DeviceIdType.MESH
        )
    pl.semaphore_wait(barrier, n_path)

    def far(d, src, dst, send, recv, c=0):
        return pltpu.make_async_remote_copy(
            src_ref=src,
            dst_ref=dst,
            send_sem=send.at[c, d - 1],
            recv_sem=recv.at[c, d - 1],
            device_id={"path": lax.rem(me + d, n_path)},
            device_id_type=pl.DeviceIdType.MESH,
        )

    def near(hop, c, src, dst):
        return pltpu.make_async_remote_copy(
            src_ref=src,
            dst_ref=dst,
            send_sem=x_send.at[hop, c],
            recv_sem=x_recv.at[hop, c],
            device_id={"inner": other},
            device_id_type=pl.DeviceIdType.MESH,
        )

    modules = held.shape[0]
    mom_copies = []
    for c, at in enumerate(strips):
        take[c].wait()

        @pl.loop(0, strip // 16)
        def _(k, c=c):
            rows_at = pl.ds(pl.multiple_of(c * strip + k * 16, 16), 16)
            for p in range(n_path):
                chosen = held[0, rows_at, :]
                for m in range(1, modules):
                    chosen = jnp.where(route_ref[p] == m, held[m, rows_at, :], chosen)
                msend[p, rows_at, :] = chosen.astype(jnp.bfloat16)
            held[:, rows_at, :] = outer_mu * held[:, rows_at, :]

        for d in range(1, n_path):
            copy = far(d, msend.at[lax.rem(me + d, n_path), at], mom.at[me, at], m_send, m_recv, c)
            copy.start()
            mom_copies.append((d, copy))
        give[c].start()
    load_m.start()

    load_x.wait()
    piece = 32
    own_at = pl.ds(pl.multiple_of(mine * rows, rows), rows)
    other_at = pl.ds(pl.multiple_of(other * rows, rows), rows)
    hop0 = []
    for c in range(chunks):

        @pl.loop(0, step // piece)
        def _(k, c=c):
            at = pl.ds(pl.multiple_of(c * step + k * piece, piece), piece)
            xf = x_v[at, :].astype(f32)
            inv = lax.rsqrt(jnp.mean(xf * xf, axis=-1, keepdims=True) + eps)
            ncols[at, :] = (x_v[at, own_at].astype(f32) * inv).astype(jnp.bfloat16)
            nsend[at, :] = (x_v[at, other_at].astype(f32) * inv).astype(jnp.bfloat16)

        at = pl.ds(c * step, step)
        copy = near(0, c, nsend.at[at], ncols.at[pl.ds(tokens + c * step, step)])
        copy.start()
        hop0.append(copy)

    load_w.wait()
    load_t.wait()

    @pl.loop(0, cols // tile)
    def _(j):
        at = pl.ds(pl.multiple_of(j * tile, tile), tile)
        part = jnp.dot(ncols[0:tokens, :], w_v[:, at], preferred_element_type=f32)
        lp[:, at] = part * scale - t_v[:, at].astype(f32)

    hop1 = []
    for c in range(chunks):
        hop0[c].wait_recv()

        @pl.loop(0, cols // tile)
        def _(j, c=c):
            at = pl.ds(pl.multiple_of(j * tile, tile), tile)
            part = jnp.dot(
                ncols[tokens + c * step : tokens + (c + 1) * step, :], w_v[:, at], preferred_element_type=f32
            )
            psend[c * step : (c + 1) * step, at] = (part * scale).astype(jnp.bfloat16)

        at = pl.ds(c * step, step)
        copy = near(1, c, psend.at[at], precv.at[at])
        copy.start()
        hop1.append(copy)

    hop2 = []
    for c in range(chunks):
        hop1[c].wait_recv()

        @pl.loop(0, step // piece)
        def _(k, c=c):
            at = pl.ds(pl.multiple_of(c * step + k * piece, piece), piece)
            resid[at, :] = (lp[at, :] + precv[at, :].astype(f32)).astype(jnp.bfloat16)

        copy = near(2, c, resid.at[pl.ds(c * step, step)], resid.at[pl.ds(tokens + c * step, step)])
        copy.start()
        hop2.append(copy)
    for copy in hop2:
        copy.wait_recv()

    delta_copies = []
    for d in list(range(1, n_path)) + [0]:
        q = lax.rem(me + d, n_path)
        left = pl.ds(pl.multiple_of(q * block, block), block)

        @pl.loop(0, cols // tile)
        def _(j, q=q, left=left):
            at = pl.ds(pl.multiple_of(j * tile, tile), tile)
            grad = lax.dot_general(
                ncols[:, left], resid[:, at], (((0,), (0,)), ((), ())), preferred_element_type=f32
            )
            delta[q, :, at] = (grad * coef).astype(jnp.bfloat16)

        if d > 0:
            copy = far(d, delta.at[q], recv_hbm.at[me], d_send, d_recv)
        else:
            copy = pltpu.make_async_copy(delta.at[q], recv_hbm.at[me], out_sem.at[0])
        copy.start()
        delta_copies.append(copy)

    out_copies = []
    for d in range(n_path):
        if d == 0:
            load_m.wait()
        else:
            for offset, copy in mom_copies:
                if offset == d:
                    copy.wait_recv()
        o = lax.rem(me + n_path - d, n_path)

        @pl.loop(0, block // piece)
        def _(k, o=o):
            at = pl.ds(pl.multiple_of(k * piece, piece), piece)
            w_at = pl.ds(pl.multiple_of(o * block + k * piece, piece), piece)
            step_delta = delta[o, at, :].astype(f32)
            velocity = outer_mu * mom[o, at, :].astype(f32) + step_delta
            update = (outer_rate * (step_delta + outer_mu * velocity)).astype(jnp.bfloat16)
            w_v[w_at, :] = (w_v[w_at, :].astype(f32) - update.astype(f32)).astype(jnp.bfloat16)

        here = pl.ds(pl.multiple_of(o * block, block), block)
        copy = pltpu.make_async_copy(w_v.at[here], new_w_hbm.at[here], out_sem.at[1 + d])
        copy.start()
        out_copies.append(copy)

    for copy in hop0 + hop1 + hop2 + [copy for _, copy in mom_copies]:
        copy.wait_send()
    for copy in give:
        copy.wait()
    for copy in delta_copies[:-1]:
        copy.wait()
    delta_copies[-1].wait()
    for copy in out_copies:
        copy.wait()


def distinct_device(route, inputs, targets, path_weights, momentum):
    n_path = lax.axis_size("path")
    tokens, width = inputs.shape[1:]
    rows, cols = path_weights.shape[1:]
    block = rows // n_path
    chunks = 2
    bf16 = jnp.bfloat16
    held = momentum[:, 0]
    route = pltpu.with_memory_space_constraint(route, pltpu.HBM)
    cuts = 8
    any_space = pl.BlockSpec(memory_space=pl.ANY)
    dma = pltpu.SemaphoreType.DMA
    new_weight, received, kept = pl.pallas_call(
        functools.partial(sync_kernel, n_path, chunks),
        out_shape=(
            jax.ShapeDtypeStruct((rows, cols), bf16),
            jax.ShapeDtypeStruct((n_path, block, cols), bf16),
            jax.ShapeDtypeStruct(held.shape, held.dtype),
        ),
        in_specs=[pl.BlockSpec(memory_space=pltpu.SMEM)] + [any_space] * 4,
        out_specs=(any_space,) * 3,
        scratch_shapes=[
            pltpu.VMEM((tokens, width), bf16),
            pltpu.VMEM((tokens, cols), bf16),
            pltpu.VMEM((rows, cols), bf16),
            pltpu.VMEM((tokens, rows), bf16),
            pltpu.VMEM((2 * tokens, rows), bf16),
            pltpu.VMEM((tokens, cols), bf16),
            pltpu.VMEM((tokens, cols), bf16),
            pltpu.VMEM((tokens, cols), jnp.float32),
            pltpu.VMEM((2 * tokens, cols), bf16),
            pltpu.VMEM((n_path, block, cols), bf16),
            pltpu.VMEM((n_path, block, cols), bf16),
            pltpu.VMEM(held.shape, held.dtype),
            pltpu.VMEM((n_path, block, cols), bf16),
            dma((4,)),
            dma((2 * cuts,)),
            dma((1 + n_path,)),
            dma((3, chunks)),
            dma((3, chunks)),
            dma((cuts, n_path - 1)),
            dma((cuts, n_path - 1)),
            dma((1, n_path - 1)),
            dma((1, n_path - 1)),
        ],
        compiler_params=pltpu.CompilerParams(
            collective_id=0, has_side_effects=True, vmem_limit_bytes=38 * 2**20
        ),
        cost_estimate=pl.CostEstimate(
            flops=8 * tokens * rows * cols, bytes_accessed=12 * rows * cols, transcendentals=0
        ),
    )(route, *[pltpu.with_memory_space_constraint(a, pltpu.HBM) for a in (inputs[0], targets[0], path_weights[0], held)])
    velocity, new_weight = next_momentum(route, kept, received, new_weight)
    return (new_weight[None], velocity[:, None])


def solution(mesh):
    placed = (
        P("groups"),
        P(("groups", "path"), "inner", None),
        P(("groups", "path"), "inner", "shard"),
        P(("groups", "path"), "inner", "shard"),
        P("groups", "inner", "path", "shard"),
    )

    def step(route, inputs, targets, path_weights, momentum):
        paths, modules = mesh.shape["path"], momentum.shape[0]
        distinct = 2 <= paths <= modules and mesh.shape["inner"] == 2
        return (distinct_device if distinct else per_device)(route, inputs, targets, path_weights, momentum)

    return jax.shard_map(
        step,
        mesh=mesh,
        in_specs=placed,
        out_specs=(P(("groups", "path"), "inner", "shard"), P("groups", "inner", "path", "shard")),
        check_vma=False,
    )
```
